32 devices in a mesh: crops: 2 (over y), row: 4 (over x, core), col: 4 (over z).
Axes of the slice: x: 2, y: 2, z: 4, core: 2. Of those that a mesh axis runs over, the one named last changes fastest.
Arguments:
- pair: float32 [192, 96, 128], P(('crops', 'row'), 'col'), parts along dimension 0, may hold values from -6 to 6
- pair_mask: int32 [192, 96], P(('crops', 'row'), 'col'), parts along dimension 0, may hold values 0 or 1
- chain_ids: int32 [192], P('crops'), parts along dimension 0, may hold values from 0 to 3, never falling along the last dimension, each value on 1 to 48 neighbouring positions
- chain_pair_table: float32 [2, 128], replicated, may hold values from -4 to 4
- norms: float32 [2, 4, 128], replicated, may hold values from 0.1 to 1.9
- w_in: bfloat16 [2, 128, 640], replicated, may hold values from -0.5 to 0.5
- w_out: bfloat16 [2, 128, 128], replicated, may hold values from -0.5 to 0.5
Outputs:
- updated: float32 [192, 96, 128], P(('crops', 'row'), 'col'), parts along dimension 0
The draws below stay inside these ranges and needn't reach their ends.
There are 2 independent parts, one for each index of `crops`. The reference program is written for one: setup_inputs(seed, part) draws one part's arguments, and reference() takes and returns one part's arrays. A program takes and returns all parts, laid end to end along the dimension named above; an argument that names none is the same for every part. Nothing has to cross between parts.
Inputs may be any that keep to these rules, and one draw needn't show every extreme that they name: `chain_ids`: chain numbers never fall along the residues; every chain holds one to 48 residues.
All inputs are finite; a program needn't handle non-finite values. No bound on the sum of `pair_mask` on one device may be relied on, other than what follows from the above.
Results may differ from the reference program's by a relative error of at most 0.0023.
Values may be sent and summed in bfloat16 or wider, within the bound.
A program may use at most 64 MiB of HBM per device.

```python
import math
import jax
import jax.numpy as jnp
import numpy as np
from jax import lax

C = 128
RES = 96


def place_ends(result, rng, smallest, largest):
    extent = result.shape
    index_at = [jax.random.randint(jax.random.fold_in(rng, axis), (), 0, extent[axis]) for axis in range(len(extent))]
    result = result.at[tuple(index_at)].set(smallest)
    longest = extent.index(max(extent))
    index_at[longest] = (index_at[longest] + 1) % extent[longest]
    return result.at[tuple(index_at)].set(largest)


def block_levels(own_key, extent, shards, smallest, top_value):
    level, own = 1.0, jax.random.fold_in(own_key, 6)
    for axis_at, shards_of in shards:
        draws = jnp.exp(jax.random.uniform(jax.random.fold_in(own, axis_at), (shards_of,), jnp.float32, smallest / len(shards), top_value / len(shards)))
        level = level * jnp.repeat(draws, extent[axis_at] // shards_of).reshape([-1 if axis == axis_at else 1 for axis in range(len(extent))])
    return level


def split_up(count, total, limit, skew):
    weights = [(1 << 20) // math.isqrt(rank ** skew) + 1 for rank in range(2, count + 1)]
    rest, holding = total - limit - (count - 1), [1] * (count - 1)
    while rest > 0:
        free = [i for i in range(count - 1) if holding[i] < limit]
        mass, left = sum([weights[i] for i in free]), rest
        for i in free:
            addition = min(limit - holding[i], max(1, left * weights[i] // mass), rest)
            holding[i] = holding[i] + addition
            rest = rest - addition
    return np.array([limit] + holding)


def ragged_sizes(rng, amount, total, bound, slope):
    if amount == 2:
        one = jax.random.randint(rng, (), max(1, total - bound), min(bound, total - 1) + 1)
        return jnp.stack([one, total - one])
    sizes = jnp.asarray(split_up(amount, total, bound, slope), jnp.int32)
    twos = (amount - 1) // 2
    giver, taker = sizes[1:1 + 2 * twos:2], sizes[2:2 + 2 * twos:2]
    room = jnp.minimum(giver - 1, bound - taker)
    moved = jax.random.randint(jax.random.fold_in(rng, 1), (twos,), 0, 1 << 20) % (room + 1)
    sizes = sizes.at[1:1 + 2 * twos:2].set(giver - moved).at[2:2 + 2 * twos:2].set(taker + moved)
    return sizes[jax.random.permutation(jax.random.fold_in(rng, 2), amount)]


def scatter_about(own_key, dims, scale, bound, shards=(), kind=jnp.bfloat16):
    values = scale * jax.random.normal(own_key, dims, jnp.float32)
    if shards:
        values = values * block_levels(own_key, dims, shards, -0.22, 0.18)
    return jnp.clip(values, -bound, bound).astype(kind)


def setup_inputs(seed: int = 0, part: int = 0) -> dict:
    splits = jax.random.split(jax.random.key(seed), 8)
    own_keys = jax.random.split(jax.random.fold_in(splits[7], part), 8)
    pair = scatter_about(own_keys[0], (RES, RES, C), 1.0, 6.0, ((0, 4), (1, 4)), jnp.float32)
    pair_mask = place_ends((jax.random.randint(own_keys[1], (RES, RES), 0, 8) < 7).astype(jnp.int32), jax.random.fold_in(own_keys[1], 1), 0, 1)
    chain_ids = jnp.searchsorted(jnp.cumsum(ragged_sizes(own_keys[2], 4, RES, RES // 2, 0)), jnp.arange(RES), side="right").astype(jnp.int32)
    chain_pair_table = scatter_about(splits[3], (2, C), 1.0, 4.0, (), jnp.float32)
    norms = jnp.clip(1.0 + 0.18 * jax.random.normal(splits[4], (2, 4, C), jnp.float32), 0.1, 1.9)
    w_in = scatter_about(splits[5], (2, C, 5 * C), C ** -0.5, 0.5)
    w_out = scatter_about(splits[6], (2, C, C), C ** -0.5, 0.5)
    return {"pair": pair, "pair_mask": pair_mask, "chain_ids": chain_ids, "chain_pair_table": chain_pair_table, "norms": norms, "w_in": w_in, "w_out": w_out}


def layer_norm(value, gain, bias):
    mean = lax.optimization_barrier(jnp.mean(value, axis=-1, keepdims=True))
    spread = lax.optimization_barrier(jnp.mean(jnp.square(value - mean), axis=-1, keepdims=True))
    return (value - mean) * jax.lax.rsqrt(spread + 1e-05) * gain + bias

def inputs_of(state, norms_one, weight_in, pair_mask):
    width = state.shape[-1]
    normed = layer_norm(state, norms_one[0], norms_one[1]).astype(jnp.bfloat16)
    projected = jnp.einsum('ijc,cd->ijd', normed.astype(jnp.float32), weight_in.astype(jnp.float32))
    masking = pair_mask.astype(jnp.float32)[..., None]
    left = (masking * jax.nn.sigmoid(projected[..., width:2 * width]) * projected[..., :width]).astype(jnp.bfloat16)
    right = (masking * jax.nn.sigmoid(projected[..., 3 * width:4 * width]) * projected[..., 2 * width:3 * width]).astype(jnp.bfloat16)
    gating = jax.nn.sigmoid(projected[..., 4 * width:])
    return (left, right, gating)

def finish(state, triangle, gating, norms_one, weight_out):
    tnorm = layer_norm(triangle, norms_one[2], norms_one[3]).astype(jnp.bfloat16)
    return state + gating * jnp.einsum('ijc,cd->ijd', tnorm.astype(jnp.float32), weight_out.astype(jnp.float32))

def reference(pair, pair_mask, chain_ids, chain_pair_table, norms, w_in, w_out):
    same = chain_ids[:, None] == chain_ids[None, :]
    state = pair + jnp.where(same[..., None], chain_pair_table[1], chain_pair_table[0])
    left, right, gating = inputs_of(state, norms[0], w_in[0], pair_mask)
    triangle = jnp.einsum('ikc,jkc->ijc', left.astype(jnp.float32), right.astype(jnp.float32))
    state = finish(state, triangle, gating, norms[0], w_out[0])
    left, right, gating = inputs_of(state, norms[1], w_in[1], pair_mask)
    triangle = jnp.einsum('kic,kjc->ijc', left.astype(jnp.float32), right.astype(jnp.float32))
    return finish(state, triangle, gating, norms[1], w_out[1])
```

```python
import functools

import jax
import jax.numpy as jnp
from jax import lax
from jax.experimental import pallas as pl
from jax.experimental.pallas import tpu as pltpu
from jax.sharding import PartitionSpec as P

F32 = jnp.float32
BF16 = jnp.bfloat16
MESH = pl.DeviceIdType.MESH
CHUNKS = 6


def xor(a, b, n):
    total = 0
    bit = 1
    while bit < n:
        x, y = (a // bit) % 2, (b // bit) % 2
        total = total + bit * (x + y - 2 * x * y)
        bit *= 2
    return total


def layer_norm(value, gain, bias):
    mean = jnp.mean(value, axis=-1, keepdims=True)
    centered = value - mean
    spread = jnp.mean(centered * centered, axis=-1, keepdims=True)
    return centered * lax.rsqrt(spread + 1e-05) * gain + bias


def products(left, right, out, size, stride_i, stride_k, group=8):
    def step(index, carry):
        first = index * group
        sums = [jnp.zeros((size, left.shape[-1]), F32) for _ in range(group)]
        for k in range(size):
            right_k = right[k * size : (k + 1) * size, :]
            for i in range(group):
                one = left[pl.ds((first + i) * stride_i + k * stride_k, 1), :]
                sums[i] = sums[i] + one * right_k
        for i in range(group):
            out[pl.ds(pl.multiple_of((first + i) * size, 8), size), :] = sums[i]
        return carry

    lax.fori_loop(0, size // group, step, 0)


def kernel(
    n,
    size,
    pair,
    mask,
    chain,
    table,
    norms,
    w_in,
    w_out,
    out,
    state,
    gating,
    masking,
    own_left,
    own_right,
    operand,
    triangle,
    total,
    right_slots,
    left_slots,
    part_one,
    part_two,
    got_one,
    got_two,
    send_right,
    recv_right,
    send_left,
    recv_left,
    send_one,
    recv_one,
    send_two,
    recv_two,
):
    row, col = lax.axis_index("row"), lax.axis_index("col")
    crop = lax.axis_index("crops")
    width = pair.shape[-1]
    rows = size * size
    piece = rows // CHUNKS

    barrier = pltpu.get_barrier_semaphore()
    for s in range(1, n):
        pl.semaphore_signal(
            barrier, inc=1, device_id=(crop, xor(row, s, n), col), device_id_type=MESH
        )
        pl.semaphore_signal(
            barrier, inc=1, device_id=(crop, row, xor(col, s, n)), device_id_type=MESH
        )

    sub = lax.broadcasted_iota(jnp.int32, (size, width), 0)
    columns = jnp.zeros((size, width), jnp.int32)
    for j in range(size):
        columns = jnp.where(sub == j, chain[col * size + j], columns)
    turned = mask[...].astype(F32).T
    for i in range(size):
        same = columns == chain[row * size + i]
        at = slice(i * size, (i + 1) * size)
        state[at, :] = pair[i] + jnp.where(same, table[1:2, :], table[0:1, :])
        masking[at, :] = jnp.broadcast_to(turned[:, i : i + 1], (size, width))

    def inputs_of(u, left_to, right_to):
        for part in range(CHUNKS):
            at = slice(part * piece, (part + 1) * piece)
            normed = layer_norm(state[at, :], norms[u, 0:1, :], norms[u, 1:2, :]).astype(BF16)
            projected = jnp.dot(normed, w_in[u], preferred_element_type=F32)
            block = [projected[:, b * width : (b + 1) * width] for b in range(5)]
            here = masking[at, :]
            left_to(part, at, here * jax.nn.sigmoid(block[1]) * block[0])
            right_to(part, at, here * jax.nn.sigmoid(block[3]) * block[2])
            gating[at, :] = jax.nn.sigmoid(block[4])

    def finish(u, put):
        for part in range(CHUNKS):
            at = slice(part * piece, (part + 1) * piece)
            tnorm = layer_norm(total[at, :], norms[u, 2:3, :], norms[u, 3:4, :]).astype(BF16)
            put(
                part,
                at,
                state[at, :]
                + gating[at, :] * jnp.dot(tnorm, w_out[u], preferred_element_type=F32),
            )

    def put_f32(ref):
        def put(part, at, value):
            ref[at, :] = value

        return put

    def put_rounded(ref):
        def put(part, at, value):
            ref[at, :] = value.astype(BF16).astype(F32)

        return put

    def copy(src, dst, send, recv, to):
        return pltpu.make_async_remote_copy(
            src_ref=src,
            dst_ref=dst,
            send_sem=send,
            recv_sem=recv,
            device_id=to,
            device_id_type=MESH,
        )

    def right_copy(s):
        return copy(
            right_slots.at[0],
            right_slots.at[s],
            send_right.at[s],
            recv_right.at[s],
            (crop, xor(row, s, n), col),
        )

    def left_copy(s):
        return copy(
            left_slots.at[0],
            left_slots.at[s],
            send_left.at[s],
            recv_left.at[s],
            (crop, row, xor(col, s, n)),
        )

    def one_copy(s):
        return copy(
            part_one.at[s], got_one.at[s], send_one.at[s], recv_one.at[s],
            (crop, row, xor(col, s, n)),
        )

    def two_copy(s):
        return copy(
            part_two.at[s], got_two.at[s], send_two.at[s], recv_two.at[s],
            (crop, xor(row, s, n), col),
        )

    inputs_of(0, put_rounded(own_left), put_f32(own_right))
    pairs = 2 * size
    for k in range(0, size, 2):
        both = [own_right[pl.ds(k + d, size, stride=size), :] for d in range(2)]
        right_slots[0, k * size : k * size + pairs, :] = jnp.concatenate(both, axis=0).astype(BF16)
    pl.semaphore_wait(barrier, 2 * (n - 1))
    for s in range(1, n):
        right_copy(s).start()

    def outgoing(s, carry):
        @pl.when(s > 0)
        def _():
            right_copy(s).wait_recv()

        operand[...] = right_slots[s].astype(F32)
        products(own_left, operand, triangle, size, size, 1)
        slot = xor(col, xor(row, s, n), n)

        @pl.when(slot == 0)
        def _():
            total[...] = triangle[...]

        @pl.when(slot > 0)
        def _():
            part_one[slot] = triangle[...].astype(BF16)
            one_copy(slot).start()

        return carry

    lax.fori_loop(0, n, outgoing, 0)
    for s in range(1, n):
        one_copy(s).wait_recv()
        total[...] += got_one[s].astype(F32)
    finish(0, put_f32(state))

    def left_to(part, at, value):
        left_slots[0, at, :] = value.astype(BF16)

    inputs_of(1, left_to, put_rounded(own_right))
    for s in range(1, n):
        left_copy(s).start()

    def incoming(s, carry):
        @pl.when(s > 0)
        def _():
            left_copy(s).wait_recv()

        operand[...] = left_slots[s].astype(F32)
        products(operand, own_right, triangle, size, 1, size)
        slot = xor(row, xor(col, s, n), n)

        @pl.when(slot == 0)
        def _():
            total[...] = triangle[...]

        @pl.when(slot > 0)
        def _():
            part_two[slot] = triangle[...].astype(BF16)
            two_copy(slot).start()

        return carry

    lax.fori_loop(0, n, incoming, 0)
    for s in range(1, n):
        two_copy(s).wait_recv()
        total[...] += got_two[s].astype(F32)

    def put_out(part, at, value):
        lines = piece // size
        out[part * lines : (part + 1) * lines] = value.reshape(lines, size, width)

    finish(1, put_out)
    for s in range(1, n):
        right_copy(s).wait_send()
        one_copy(s).wait_send()
        left_copy(s).wait_send()
        two_copy(s).wait_send()


def body(pair, pair_mask, chain_ids, chain_pair_table, norms, w_in, w_out):
    n = lax.axis_size("row")
    size, _, width = pair.shape
    rows = size * size
    vmem = pl.BlockSpec(memory_space=pltpu.VMEM)
    smem = pl.BlockSpec(memory_space=pltpu.SMEM)
    flat = pltpu.VMEM((rows, width), F32)
    slots = pltpu.VMEM((n, rows, width), BF16)
    return pl.pallas_call(
        functools.partial(kernel, n, size),
        out_shape=jax.ShapeDtypeStruct(pair.shape, F32),
        in_specs=[vmem, vmem, smem, vmem, vmem, vmem, vmem],
        out_specs=vmem,
        scratch_shapes=[flat] * 8 + [slots] * 6 + [pltpu.SemaphoreType.DMA((n,))] * 8,
        compiler_params=pltpu.CompilerParams(
            collective_id=0, has_side_effects=True, vmem_limit_bytes=40 * 1024 * 1024
        ),
    )(pair, pair_mask, chain_ids, chain_pair_table, norms, w_in, w_out)


def solution(mesh):
    placed = (
        P(("crops", "row"), "col", None),
        P(("crops", "row"), "col"),
        P("crops"),
        P(),
        P(),
        P(),
        P(),
    )
    return jax.shard_map(
        body,
        mesh=mesh,
        in_specs=placed,
        out_specs=P(("crops", "row"), "col", None),
        check_vma=False,
    )
```

```python
import functools

import jax
import jax.numpy as jnp
from jax import lax
from jax.experimental import pallas as pl
from jax.experimental.pallas import tpu as pltpu
from jax.sharding import PartitionSpec as P

F32 = jnp.float32
BF16 = jnp.bfloat16
MESH = pl.DeviceIdType.MESH
LINES = 8


def xor(a, b, n):
    total = 0
    bit = 1
    while bit < n:
        x, y = (a // bit) % 2, (b // bit) % 2
        total = total + bit * (x + y - 2 * x * y)
        bit *= 2
    return total


def layer_norm(value, gain, bias):
    mean = jnp.mean(value, axis=-1, keepdims=True)
    centered = value - mean
    spread = jnp.mean(centered * centered, axis=-1, keepdims=True)
    return centered * lax.rsqrt(spread + 1e-05) * gain + bias


def kernel(
    n,
    size,
    pair_hbm,
    mask_hbm,
    chain_hbm,
    table_hbm,
    norms_hbm,
    w_in_hbm,
    w_out_hbm,
    out,
    pair,
    mask,
    chain,
    table,
    norms,
    w_in,
    w_out,
    normed,
    state,
    gating,
    masking,
    own_left,
    own_right,
    operand,
    triangle,
    total,
    right_slots,
    left_slots,
    part_one,
    part_two,
    got_one,
    got_two,
    load,
    send_right,
    recv_right,
    send_left,
    recv_left,
    send_one,
    recv_one,
    send_two,
    recv_two,
):
    row, col = lax.axis_index("row"), lax.axis_index("col")
    crop = lax.axis_index("crops")
    width = pair.shape[-1]
    count = size // LINES
    piece = size * LINES
    part = LINES * LINES

    loads = [
        pltpu.make_async_copy(source, target, load.at[index])
        for index, (source, target) in enumerate(
            (
                (pair_hbm, pair),
                (mask_hbm, mask),
                (chain_hbm, chain),
                (table_hbm, table),
                (norms_hbm, norms),
                (w_in_hbm, w_in),
                (w_out_hbm, w_out),
            )
        )
    ]
    for one in loads:
        one.start()

    barrier = pltpu.get_barrier_semaphore()
    for s in range(1, n):
        pl.semaphore_signal(
            barrier, inc=1, device_id=(crop, xor(row, s, n), col), device_id_type=MESH
        )
        pl.semaphore_signal(
            barrier, inc=1, device_id=(crop, row, xor(col, s, n)), device_id_type=MESH
        )

    def at(q):
        return slice(q * piece, (q + 1) * piece)

    def copy(slots_from, s_from, slots_to, s, q, send, recv, to):
        return pltpu.make_async_remote_copy(
            src_ref=slots_from.at[s_from, pl.ds(q * piece, piece), :],
            dst_ref=slots_to.at[s, pl.ds(q * piece, piece), :],
            send_sem=send.at[q, s],
            recv_sem=recv.at[q, s],
            device_id=to,
            device_id_type=MESH,
        )

    def along_row(s):
        return (crop, xor(row, s, n), col)

    def along_col(s):
        return (crop, row, xor(col, s, n))

    def right_copy(q, s):
        return copy(right_slots, 0, right_slots, s, q, send_right, recv_right, along_row(s))

    def left_copy(q, s):
        return copy(left_slots, 0, left_slots, s, q, send_left, recv_left, along_col(s))

    def one_copy(q, s):
        return copy(part_one, s, got_one, s, q, send_one, recv_one, along_col(s))

    def two_copy(q, s):
        return copy(part_two, s, got_two, s, q, send_two, recv_two, along_row(s))

    for index in (2, 1, 3, 0):
        loads[index].wait()
    sub = lax.broadcasted_iota(jnp.int32, (size, width), 0)
    columns = jnp.zeros((size, width), jnp.int32)
    for j in range(size):
        columns = jnp.where(sub == j, chain[col * size + j], columns)
    turned = mask[...].astype(F32).T
    for i in range(size):
        same = columns == chain[row * size + i]
        begin = pair[i] + jnp.where(same, table[1:2, :], table[0:1, :])
        held = jnp.broadcast_to(turned[:, i : i + 1], (size, width))
        for q in range(count):
            here = slice(q * piece + i * LINES, q * piece + (i + 1) * LINES)
            state[here, :] = begin[q * LINES : (q + 1) * LINES]
            masking[here, :] = held[q * LINES : (q + 1) * LINES]
    loads[4].wait()
    loads[5].wait()

    def norm(u, q):
        for half in range(2):
            h = slice(q * piece + half * (piece // 2), q * piece + (half + 1) * (piece // 2))
            normed[h, :] = layer_norm(state[h, :], norms[u, 0:1, :], norms[u, 1:2, :]).astype(BF16)

    def value_of(u, q, first):
        both = jnp.dot(
            normed[at(q), :],
            w_in[u, :, first * width : (first + 2) * width],
            preferred_element_type=F32,
        )
        return masking[at(q), :] * jax.nn.sigmoid(both[:, width:]) * both[:, :width]

    def gate_of(u, q):
        gating[at(q), :] = jax.nn.sigmoid(
            jnp.dot(normed[at(q), :], w_in[u, :, 4 * width :], preferred_element_type=F32)
        )

    def updated(u, where):
        tnorm = layer_norm(total[where, :], norms[u, 2:3, :], norms[u, 3:4, :]).astype(BF16)
        moved = jnp.dot(tnorm, w_out[u], preferred_element_type=F32)
        return state[where, :] + gating[where, :] * moved

    for q in range(count):
        norm(0, q)
        own_right[at(q), :] = value_of(0, q, 2)
    for q in range(count):
        for k in range(0, size, 2):
            both = [
                own_right[
                    pl.ds((k + d) // LINES * piece + q * part + (k + d) % LINES, LINES, stride=LINES), :
                ]
                for d in range(2)
            ]
            right_slots[0, q * piece + k * LINES : q * piece + (k + 2) * LINES, :] = (
                jnp.concatenate(both, axis=0).astype(BF16)
            )
        if q == 0:
            pl.semaphore_wait(barrier, 2 * (n - 1))
        for s in range(1, n):
            right_copy(q, s).start()
    for q in range(count):
        own_left[at(q), :] = value_of(0, q, 0).astype(BF16).astype(F32)
        gate_of(0, q)
    loads[6].wait()

    def outgoing(q):
        def step(s, carry):
            @pl.when(s > 0)
            def _():
                right_copy(q, s).wait_recv()

            operand[...] = right_slots[s, at(q), :].astype(F32)
            sums = [jnp.zeros((LINES, width), F32) for _ in range(size)]
            for k in range(size):
                right_k = operand[k * LINES : (k + 1) * LINES, :]
                for i in range(size):
                    line = k // LINES * piece + i * LINES + k % LINES
                    sums[i] = sums[i] + own_left[line : line + 1, :] * right_k
            for i in range(size):
                triangle[i * LINES : (i + 1) * LINES, :] = sums[i]
            slot = xor(col, xor(row, s, n), n)

            @pl.when(slot == 0)
            def _():
                total[at(q), :] = triangle[...]

            @pl.when(slot > 0)
            def _():
                part_one[slot, at(q), :] = triangle[...].astype(BF16)
                one_copy(q, slot).start()

            return carry

        lax.fori_loop(0, n, step, 0)

    def between(q):
        for s in range(1, n):
            one_copy(q, s).wait_recv()
        whole = total[at(q), :]
        for s in range(1, n):
            whole = whole + got_one[s, at(q), :].astype(F32)
        total[at(q), :] = whole
        state[at(q), :] = updated(0, at(q))
        norm(1, q)
        left_slots[0, at(q), :] = value_of(1, q, 0).astype(BF16)
        for s in range(1, n):
            left_copy(q, s).start()
        own_right[at(q), :] = value_of(1, q, 2).astype(BF16).astype(F32)
        gate_of(1, q)

    for q in range(count):
        outgoing(q)
        if q > 0:
            between(q - 1)
    between(count - 1)

    def incoming(q):
        def step(s, carry):
            @pl.when(s > 0)
            def _():
                left_copy(q, s).wait_recv()

            operand[...] = left_slots[s, at(q), :].astype(F32)
            sums = [[jnp.zeros((LINES, width), F32) for _ in range(LINES)] for _ in range(count)]
            for k in range(size):
                for b in range(count):
                    right_k = own_right[b * piece + k * LINES : b * piece + (k + 1) * LINES, :]
                    for i in range(LINES):
                        line = k * LINES + i
                        sums[b][i] = sums[b][i] + operand[line : line + 1, :] * right_k
            for b in range(count):
                for i in range(LINES):
                    to = b * part + i * LINES
                    triangle[to : to + LINES, :] = sums[b][i]
            slot = xor(row, xor(col, s, n), n)

            @pl.when(slot == 0)
            def _():
                for b in range(count):
                    to = b * piece + q * part
                    total[to : to + part, :] = triangle[b * part : (b + 1) * part, :]

            @pl.when(slot > 0)
            def _():
                part_two[slot, at(q), :] = triangle[...].astype(BF16)
                two_copy(q, slot).start()

            return carry

        lax.fori_loop(0, n, step, 0)

    def last(q):
        for s in range(1, n):
            two_copy(q, s).wait_recv()
        for b in range(count):
            to = slice(b * piece + q * part, b * piece + (q + 1) * part)
            whole = total[to, :]
            for s in range(1, n):
                begin = q * piece + b * part
                whole = whole + got_two[s, begin : begin + part, :].astype(F32)
            total[to, :] = whole
            out[q * LINES : (q + 1) * LINES, b * LINES : (b + 1) * LINES, :] = updated(
                1, to
            ).reshape(LINES, LINES, width)

    for q in range(count):
        incoming(q)
        if q > 0:
            last(q - 1)
    last(count - 1)
    for q in range(count):
        for s in range(1, n):
            right_copy(q, s).wait_send()
            one_copy(q, s).wait_send()
            left_copy(q, s).wait_send()
            two_copy(q, s).wait_send()


def body(pair, pair_mask, chain_ids, chain_pair_table, norms, w_in, w_out):
    n = lax.axis_size("row")
    size, _, width = pair.shape
    rows = size * size
    anywhere = pl.BlockSpec(memory_space=pl.ANY)
    flat = pltpu.VMEM((rows, width), F32)
    few = pltpu.VMEM((size * LINES, width), F32)
    slots = pltpu.VMEM((n, rows, width), BF16)
    inputs = (pair, pair_mask, chain_ids, chain_pair_table, norms, w_in, w_out)
    held = [
        (pltpu.SMEM if each is chain_ids else pltpu.VMEM)(each.shape, each.dtype)
        for each in inputs
    ]
    return pl.pallas_call(
        functools.partial(kernel, n, size),
        out_shape=jax.ShapeDtypeStruct(pair.shape, F32),
        in_specs=[anywhere] * len(inputs),
        out_specs=pl.BlockSpec(memory_space=pltpu.VMEM),
        scratch_shapes=held
        + [pltpu.VMEM((rows, width), BF16)]
        + [flat] * 5
        + [few] * 2
        + [flat]
        + [slots] * 6
        + [pltpu.SemaphoreType.DMA((len(inputs),))]
        + [pltpu.SemaphoreType.DMA((size // LINES, n))] * 8,
        compiler_params=pltpu.CompilerParams(
            collective_id=0, has_side_effects=True, vmem_limit_bytes=60 * 1024 * 1024
        ),
    )(*inputs)


def solution(mesh):
    placed = (
        P(("crops", "row"), "col", None),
        P(("crops", "row"), "col"),
        P("crops"),
        P(),
        P(),
        P(),
        P(),
    )
    return jax.shard_map(
        body,
        mesh=mesh,
        in_specs=placed,
        out_specs=P(("crops", "row"), "col", None),
        check_vma=False,
    )
```

```python
import functools

import jax
import jax.numpy as jnp
from jax import lax
from jax.experimental import pallas as pl
from jax.experimental.pallas import tpu as pltpu
from jax.sharding import PartitionSpec as P

F32 = jnp.float32
BF16 = jnp.bfloat16
MESH = pl.DeviceIdType.MESH
LINES = 8


def xor(a, b, n):
    total = 0
    bit = 1
    while bit < n:
        x, y = (a // bit) % 2, (b // bit) % 2
        total = total + bit * (x + y - 2 * x * y)
        bit *= 2
    return total


def layer_norm(value, gain, bias):
    mean = jnp.mean(value, axis=-1, keepdims=True)
    centered = value - mean
    spread = jnp.mean(centered * centered, axis=-1, keepdims=True)
    return centered * lax.rsqrt(spread + 1e-05) * gain + bias


def kernel(
    n,
    size,
    pair_hbm,
    mask_hbm,
    chain_hbm,
    table_hbm,
    norms_hbm,
    w_in_hbm,
    w_out_hbm,
    out,
    pair,
    mask,
    chain,
    table,
    norms,
    w_in,
    w_out,
    normed,
    state,
    gating,
    masking,
    own_left,
    own_right,
    operand,
    triangle,
    total,
    kept,
    right_slots,
    left_slots,
    part_one,
    part_two,
    got_one,
    got_two,
    load,
    send_right,
    recv_right,
    send_left,
    recv_left,
    send_one,
    recv_one,
    send_two,
    recv_two,
):
    row, col = lax.axis_index("row"), lax.axis_index("col")
    crop = lax.axis_index("crops")
    width = pair.shape[-1]
    count = size // LINES
    piece = size * LINES
    part = LINES * LINES

    loads = [
        pltpu.make_async_copy(source, target, load.at[index])
        for index, (source, target) in enumerate(
            (
                (pair_hbm, pair),
                (mask_hbm, mask),
                (chain_hbm, chain),
                (table_hbm, table),
                (norms_hbm, norms),
                (w_in_hbm, w_in),
                (w_out_hbm, w_out),
            )
        )
    ]
    for one in loads:
        one.start()

    barrier = pltpu.get_barrier_semaphore()
    for s in range(1, n):
        pl.semaphore_signal(
            barrier, inc=1, device_id=(crop, xor(row, s, n), col), device_id_type=MESH
        )
        pl.semaphore_signal(
            barrier, inc=1, device_id=(crop, row, xor(col, s, n)), device_id_type=MESH
        )

    def at(q):
        return slice(q * piece, (q + 1) * piece)

    def copy(slots_from, s_from, slots_to, s, q, send, recv, to):
        return pltpu.make_async_remote_copy(
            src_ref=slots_from.at[s_from, pl.ds(q * piece, piece), :],
            dst_ref=slots_to.at[s, pl.ds(q * piece, piece), :],
            send_sem=send.at[q, s],
            recv_sem=recv.at[q, s],
            device_id=to,
            device_id_type=MESH,
        )

    def along_row(s):
        return (crop, xor(row, s, n), col)

    def along_col(s):
        return (crop, row, xor(col, s, n))

    def right_copy(q, s):
        return copy(right_slots, 0, right_slots, s, q, send_right, recv_right, along_row(s))

    def left_copy(q, s):
        if s > 1 and s % 2 == 1:
            return copy(
                left_slots, s - 1, left_slots, s, q, send_left, recv_left, along_col(1)
            )
        return copy(left_slots, 0, left_slots, s, q, send_left, recv_left, along_col(s))

    def landed(q, s):
        return copy(left_slots, 0, left_slots, s, q, send_left, recv_left, along_col(1))

    def near_copy(q, s):
        return copy(part_one, s, got_one, s, q, send_one, recv_one, along_col(1))

    def far_copy(q, s):
        return copy(part_one, s, got_one, s, q, send_one, recv_one, along_col(s))

    def two_copy(q, s):
        return copy(part_two, s, got_two, s, q, send_two, recv_two, along_row(s))

    for index in (2, 1, 3, 0):
        loads[index].wait()
    sub = lax.broadcasted_iota(jnp.int32, (size, width), 0)
    columns = jnp.zeros((size, width), jnp.int32)
    for j in range(size):
        columns = jnp.where(sub == j, chain[col * size + j], columns)
    turned = mask[...].astype(F32).T
    for i in range(size):
        same = columns == chain[row * size + i]
        begin = pair[i] + jnp.where(same, table[1:2, :], table[0:1, :])
        held = jnp.broadcast_to(turned[:, i : i + 1], (size, width))
        for q in range(count):
            here = slice(q * piece + i * LINES, q * piece + (i + 1) * LINES)
            state[here, :] = begin[q * LINES : (q + 1) * LINES]
            masking[here, :] = held[q * LINES : (q + 1) * LINES]
    loads[4].wait()
    loads[5].wait()

    def norm(u, q):
        for half in range(2):
            h = slice(q * piece + half * (piece // 2), q * piece + (half + 1) * (piece // 2))
            normed[h, :] = layer_norm(state[h, :], norms[u, 0:1, :], norms[u, 1:2, :]).astype(BF16)

    def value_of(u, q, first):
        both = jnp.dot(
            normed[at(q), :],
            w_in[u, :, first * width : (first + 2) * width],
            preferred_element_type=F32,
        )
        return masking[at(q), :] * jax.nn.sigmoid(both[:, width:]) * both[:, :width]

    def gate_of(u, q):
        gating[at(q), :] = jax.nn.sigmoid(
            jnp.dot(normed[at(q), :], w_in[u, :, 4 * width :], preferred_element_type=F32)
        )

    def updated(u, where):
        tnorm = layer_norm(total[where, :], norms[u, 2:3, :], norms[u, 3:4, :]).astype(BF16)
        moved = jnp.dot(tnorm, w_out[u], preferred_element_type=F32)
        return state[where, :] + gating[where, :] * moved

    for q in range(count):
        norm(0, q)
        own_right[at(q), :] = value_of(0, q, 2)
    for q in range(count):
        for k in range(0, size, 2):
            both = [
                own_right[
                    pl.ds((k + d) // LINES * piece + q * part + (k + d) % LINES, LINES, stride=LINES), :
                ]
                for d in range(2)
            ]
            right_slots[0, q * piece + k * LINES : q * piece + (k + 2) * LINES, :] = (
                jnp.concatenate(both, axis=0).astype(BF16)
            )
        if q == 0:
            pl.semaphore_wait(barrier, 2 * (n - 1))
        for s in range(1, n):
            right_copy(q, s).start()
    for q in range(count):
        own_left[at(q), :] = value_of(0, q, 0).astype(BF16).astype(F32)
        gate_of(0, q)
    loads[6].wait()

    def outgoing(q):
        def step(s, carry):
            @pl.when(s > 0)
            def _():
                right_copy(q, s).wait_recv()

            operand[...] = right_slots[s, at(q), :].astype(F32)
            sums = [jnp.zeros((LINES, width), F32) for _ in range(size)]
            for k in range(size):
                right_k = operand[k * LINES : (k + 1) * LINES, :]
                for i in range(size):
                    line = k // LINES * piece + i * LINES + k % LINES
                    sums[i] = sums[i] + own_left[line : line + 1, :] * right_k
            for i in range(size):
                triangle[i * LINES : (i + 1) * LINES, :] = sums[i]
            slot = xor(col, xor(row, s, n), n)

            @pl.when(slot == 0)
            def _():
                total[at(q), :] = triangle[...]

            @pl.when(slot % 2 == 1)
            def _():
                part_one[slot, at(q), :] = triangle[...].astype(BF16)
                near_copy(q, slot).start()

            @pl.when(jnp.logical_and(slot > 0, slot % 2 == 0))
            def _():
                kept[slot // 2, at(q), :] = triangle[...]

            return carry

        lax.fori_loop(0, n, step, 0)

    def combine(q):
        for s in range(2, n, 2):
            near_copy(q, s + 1).wait_recv()
            both = kept[s // 2, at(q), :] + got_one[s + 1, at(q), :].astype(F32)
            part_one[s, at(q), :] = both.astype(BF16)
            far_copy(q, s).start()

    def forward(q):
        for s in range(2, n, 2):
            left_copy(q, s).wait_recv()
            left_copy(q, s + 1).start()

    def between(q):
        near_copy(q, 1).wait_recv()
        whole = total[at(q), :] + got_one[1, at(q), :].astype(F32)
        for s in range(2, n, 2):
            far_copy(q, s).wait_recv()
            whole = whole + got_one[s, at(q), :].astype(F32)
        total[at(q), :] = whole
        state[at(q), :] = updated(0, at(q))
        norm(1, q)
        left_slots[0, at(q), :] = value_of(1, q, 0).astype(BF16)
        for s in [1] + list(range(2, n, 2)):
            left_copy(q, s).start()
        own_right[at(q), :] = value_of(1, q, 2).astype(BF16).astype(F32)
        gate_of(1, q)

    outgoing(0)
    for q in range(1, count):
        outgoing(q)
        combine(q - 1)
        if q > 1:
            between(q - 2)
    combine(count - 1)
    for q in range(max(count - 2, 0), count):
        between(q)
        if q > 0:
            forward(q - 1)

    def incoming(q):
        def step(s, carry):
            @pl.when(s % 2 == 1)
            def _():
                landed(q, s).wait_recv()

            operand[...] = left_slots[s, at(q), :].astype(F32)
            sums = [[jnp.zeros((LINES, width), F32) for _ in range(LINES)] for _ in range(count)]
            for k in range(size):
                for b in range(count):
                    right_k = own_right[b * piece + k * LINES : b * piece + (k + 1) * LINES, :]
                    for i in range(LINES):
                        line = k * LINES + i
                        sums[b][i] = sums[b][i] + operand[line : line + 1, :] * right_k
            for b in range(count):
                for i in range(LINES):
                    to = b * part + i * LINES
                    triangle[to : to + LINES, :] = sums[b][i]
            slot = xor(row, xor(col, s, n), n)

            @pl.when(slot == 0)
            def _():
                for b in range(count):
                    to = b * piece + q * part
                    total[to : to + part, :] = triangle[b * part : (b + 1) * part, :]

            @pl.when(slot > 0)
            def _():
                part_two[slot, at(q), :] = triangle[...].astype(BF16)
                two_copy(q, slot).start()

            return carry

        lax.fori_loop(0, n, step, 0)

    def last(q):
        for s in range(1, n):
            two_copy(q, s).wait_recv()
        for b in range(count):
            to = slice(b * piece + q * part, b * piece + (q + 1) * part)
            whole = total[to, :]
            for s in range(1, n):
                begin = q * piece + b * part
                whole = whole + got_two[s, begin : begin + part, :].astype(F32)
            total[to, :] = whole
            out[q * LINES : (q + 1) * LINES, b * LINES : (b + 1) * LINES, :] = updated(
                1, to
            ).reshape(LINES, LINES, width)

    for q in range(count):
        incoming(q)
        if q == 0:
            forward(count - 1)
        else:
            last(q - 1)
    last(count - 1)
    for q in range(count):
        for s in range(1, n):
            right_copy(q, s).wait_send()
            near_copy(q, s).wait_send()
            left_copy(q, s).wait_send()
            two_copy(q, s).wait_send()


def body(pair, pair_mask, chain_ids, chain_pair_table, norms, w_in, w_out):
    n = lax.axis_size("row")
    size, _, width = pair.shape
    rows = size * size
    anywhere = pl.BlockSpec(memory_space=pl.ANY)
    flat = pltpu.VMEM((rows, width), F32)
    few = pltpu.VMEM((size * LINES, width), F32)
    slots = pltpu.VMEM((n, rows, width), BF16)
    inputs = (pair, pair_mask, chain_ids, chain_pair_table, norms, w_in, w_out)
    held = [
        (pltpu.SMEM if each is chain_ids else pltpu.VMEM)(each.shape, each.dtype)
        for each in inputs
    ]
    return pl.pallas_call(
        functools.partial(kernel, n, size),
        out_shape=jax.ShapeDtypeStruct(pair.shape, F32),
        in_specs=[anywhere] * len(inputs),
        out_specs=pl.BlockSpec(memory_space=pltpu.VMEM),
        scratch_shapes=held
        + [pltpu.VMEM((rows, width), BF16)]
        + [flat] * 5
        + [few] * 2
        + [flat]
        + [pltpu.VMEM((max(n // 2, 1), rows, width), F32)]
        + [slots] * 6
        + [pltpu.SemaphoreType.DMA((len(inputs),))]
        + [pltpu.SemaphoreType.DMA((size // LINES, n))] * 8,
        compiler_params=pltpu.CompilerParams(
            collective_id=0, has_side_effects=True, vmem_limit_bytes=60 * 1024 * 1024
        ),
    )(*inputs)


def solution(mesh):
    placed = (
        P(("crops", "row"), "col", None),
        P(("crops", "row"), "col"),
        P("crops"),
        P(),
        P(),
        P(),
        P(),
    )
    return jax.shard_map(
        body,
        mesh=mesh,
        in_specs=placed,
        out_specs=P(("crops", "row"), "col", None),
        check_vma=False,
    )
```
